768 devices in a mesh: row: 16 (over y, core), col: 4 (over x), dep: 12 (over z).
Axes of the slice: x: 4, y: 8, z: 12, core: 2. Of those that a mesh axis runs over, the one named last changes fastest.
Arguments:
- b_tensor: bfloat16 [12, 24576, 3072], P(None, 'row', 'dep'), may hold values from -6 to 6
- occ_green: bfloat16 [3072, 512], P('dep', 'col'), may hold values from -0.15625 to 0.15625
- virt_green: bfloat16 [24576, 512], P('row'), may hold values from -0.0546875 to 0.0546875
- mu_atom: int32 [96], replicated, may hold values from 0 to 95, as said below
- mu_target: int32 [96], replicated, may hold values from 0 to 95, as said below
- mu_sizes: int32 [96], replicated, may hold values from 64 to 200, as said below
- nu_sizes: int32 [12], P('dep'), may hold values from 64 to 200, as said below
- screen: int32 [96, 12], P(None, 'dep'), may hold values 0 or 1
Outputs:
- second_mapping: float32 [512, 12, 512], P('row', 'dep', 'col')
The draws below stay inside these ranges and needn't reach their ends.
Inputs may be any that keep to these rules, and one draw needn't show every extreme that they name: mu_target is a permutation of the block slots. Of the 6 slots a' with a' // 6 equal to one row index, at most 1 have target[a'] // 6 equal to one row index, and exactly 1 do for some such pair in every draw. mu_atom is a permutation of the atom blocks. `mu_sizes`: both ends are reached in every draw. `nu_sizes`: both ends are reached in every draw.
All inputs are finite; a program needn't handle non-finite values. No bound on the sum of `screen` on one device may be relied on, other than what follows from the above.
Results may differ from the reference program's by a relative error of at most 0.015.
Values may be sent and summed in bfloat16 or wider, within the bound.
A program may use at most 64 MiB of HBM per device.

```python
import jax
import jax.numpy as jnp
from jax import lax

BS = 256
NB_DEV = 6
NBN_DEV = 1
CAP = 1
NBMU = 96
NBNU = 12
MU = 24576
NU = 3072
NP = 12
LAM = 512
SIG = 512
N_ROW = 16
N_DEP = 12


def routing_tables(key):
    atoms = jax.random.permutation(jax.random.fold_in(key, 11), NBMU).astype(jnp.int32)
    rows = jax.random.permutation(jax.random.fold_in(key, 12), N_ROW).astype(jnp.int32)
    order = jax.random.permutation(jax.random.fold_in(key, 13), NB_DEV).astype(jnp.int32)
    inside = jax.random.permutation(jax.random.fold_in(key, 14), NB_DEV).astype(jnp.int32)
    shifts = jnp.take(rows, order // CAP)
    slots = jnp.arange(NBMU, dtype=jnp.int32)
    source = slots // NB_DEV
    within = slots % NB_DEV
    slot_target = (source + jnp.take(shifts, within)) % N_ROW * NB_DEV + jnp.take(inside, within)
    target = jnp.zeros((NBMU,), jnp.int32).at[atoms].set(slot_target)
    return (atoms, target)


def block_sizes(key, count):
    lowest = BS // 4
    highest = BS * 25 // 32
    sizes = jax.random.randint(jax.random.fold_in(key, 1), (count,), lowest, highest + 1).astype(jnp.int32)
    first = jax.random.randint(jax.random.fold_in(key, 2), (), 0, count)
    offset = jax.random.randint(jax.random.fold_in(key, 3), (), 1, count)
    second = (first + offset) % count
    places = jnp.arange(count)
    sizes = jnp.where(places == first, highest, sizes)
    return jnp.where(places == second, lowest, sizes).astype(jnp.int32)


def draw_mu_atom(key, part):
    tables = routing_tables(key)
    return tables[0]


def draw_mu_target(key, part):
    tables = routing_tables(key)
    return tables[1]


def draw_mu_sizes(key, part):
    key = jax.random.fold_in(key, 21)
    return block_sizes(key, NBMU)


def draw_nu_sizes(key, part):
    key = jax.random.fold_in(key, 22)
    return block_sizes(key, NBNU)


def set_ends(values, own_key, smallest, high):
    spot = [jax.random.randint(jax.random.fold_in(own_key, axis), (), 0, length) for axis, length in enumerate(values.shape)]
    main_axis = values.shape.index(max(values.shape))
    neighbour = spot[:main_axis] + [(spot[main_axis] + 1) % values.shape[main_axis]] + spot[main_axis + 1:]
    return values.at[tuple(spot)].set(smallest).at[tuple(neighbour)].set(high)


def steps_of(rng, shape, pieces, smallest, top_value):
    gain = 1.0
    for axis_at, blocks in pieces:
        heights = jax.random.uniform(jax.random.fold_in(jax.random.fold_in(rng, 6), axis_at), (blocks,), jnp.float32, smallest / len(pieces), top_value / len(pieces))
        gain = gain * jnp.repeat(jnp.exp(heights), shape[axis_at] // blocks).reshape((-1,) + (1,) * (len(shape) - 1 - axis_at))
    return gain


def scatter_about(stream_key, extent, scale, reach, pieces=(), kind=jnp.bfloat16):
    drawn = scale * jax.random.normal(stream_key, extent, jnp.float32)
    if pieces:
        drawn = drawn * steps_of(stream_key, extent, pieces, -0.22, 0.18)
    return jnp.clip(drawn, -reach, reach).astype(kind)


def setup_inputs(seed: int = 0) -> dict:
    splits = jax.random.split(jax.random.key(seed), 9)
    b_tensor = scatter_about(splits[0], (NP, MU, NU), 1.0, 6.0, ((1, 16), (2, 12)))
    occ_green = scatter_about(splits[1], (NU, LAM), (NU // 2) ** -0.5, 0.15625, ((0, 12), (1, 4)))
    virt_green = scatter_about(splits[2], (MU, SIG), (MU // 2) ** -0.5, 0.0546875, ((0, 16),))
    mu_atom = draw_mu_atom(jax.random.fold_in(splits[8], 71), 0)
    mu_target = draw_mu_target(jax.random.fold_in(splits[8], 71), 0)
    mu_sizes = draw_mu_sizes(jax.random.fold_in(splits[8], 71), 0)
    nu_sizes = draw_nu_sizes(jax.random.fold_in(splits[8], 71), 0)
    screen = set_ends((jax.random.randint(splits[7], (NBMU, NBNU), 0, 2) < 1).astype(jnp.int32), jax.random.fold_in(splits[7], 1), 0, 1)
    return dict(b_tensor=b_tensor, occ_green=occ_green, virt_green=virt_green, mu_atom=mu_atom, mu_target=mu_target, mu_sizes=mu_sizes, nu_sizes=nu_sizes, screen=screen)


def reference(b_tensor, occ_green, virt_green, mu_atom, mu_target, mu_sizes, nu_sizes, screen):
    inner = jnp.arange(BS, dtype=jnp.int32)
    atoms = mu_atom.astype(jnp.int32)
    mu_len = jnp.take(mu_sizes, atoms)
    row_keep = (inner[None, :] < mu_len[:, None]).astype(jnp.float32)
    col_keep = (inner[None, :] < nu_sizes[:, None]).astype(jnp.float32)
    block_keep = jnp.take(screen, atoms, axis=0).astype(jnp.float32)
    group_cols = NBN_DEV * BS

    def add_group(group, total):
        start = (group * group_cols).astype(jnp.int32)
        piece = lax.dynamic_slice_in_dim(b_tensor, start, group_cols, 2)
        cols = lax.dynamic_slice_in_dim(col_keep, (group * NBN_DEV).astype(jnp.int32), NBN_DEV, 0)
        blocks = lax.dynamic_slice_in_dim(block_keep, (group * NBN_DEV).astype(jnp.int32), NBN_DEV, 1)
        keep = row_keep[:, :, None, None] * blocks[:, None, :, None] * cols[None, None, :, :]
        keep = keep.reshape(MU, group_cols).astype(jnp.bfloat16)
        masked = (piece * keep[None]).reshape(NP * MU, group_cols)
        rows = lax.dynamic_slice_in_dim(occ_green, start, group_cols, 0)
        term = jnp.dot(masked, rows, preferred_element_type=jnp.float32)
        return total + term.astype(jnp.bfloat16).astype(jnp.float32)

    total = lax.fori_loop(0, N_DEP, add_group, jnp.zeros((NP * MU, LAM), jnp.float32))
    first = total.astype(jnp.bfloat16).reshape(NP, MU, LAM)
    target = jnp.take(mu_target, atoms).astype(jnp.int32)
    picked = jnp.take(virt_green.reshape(NBMU, BS, SIG), target, axis=0).reshape(MU, SIG)
    flat = first.transpose(1, 0, 2).reshape(MU, NP * LAM)
    result = lax.dot_general(picked, flat, (((0,), (0,)), ((), ())), preferred_element_type=jnp.float32)
    return result.reshape(SIG, NP, LAM).astype(jnp.float32)
```

```python
import functools

import jax
import jax.numpy as jnp
from jax import lax
from jax.experimental import pallas as pl
from jax.experimental.pallas import tpu as pltpu
from jax.sharding import PartitionSpec as P

MESH = pl.DeviceIdType.MESH
BF16 = jnp.bfloat16
F32 = jnp.float32

BS = 256
NB = 6
KEPT = 208
NROW, NCOL, NDEP = 16, 4, 12
NY = NROW // 2
NP = 12
SIG = 512
GROUPS = 3
P_GROUP = NP // GROUPS
ROWS_GROUP = P_GROUP * 8


def wrap(value, size):
    return jnp.where(value >= size, value - size, value)


def kernel(
    atom_ref,
    target_ref,
    size_ref,
    nu_ref,
    screen_ref,
    b_ref,
    virt_ref,
    occ_ref,
    out_ref,
    b_buf,
    virt_buf,
    occ_buf,
    picked,
    green_out,
    green_in,
    y_buf,
    y_pair,
    y_out,
    y_in,
    w_out,
    w_in,
    x_out,
    b_sem,
    local_sem,
    green_send,
    green_recv,
    occ_send,
    occ_recv,
    pair_send,
    pair_recv,
    y_send,
    y_recv,
    w_send,
    w_recv,
    x_send,
    x_recv,
):
    row, col, dep = lax.axis_index("row"), lax.axis_index("col"), lax.axis_index("dep")
    core = lax.rem(row, 2)
    y = lax.div(row, 2)
    other = 1 - core

    virt_copy = pltpu.make_async_copy(virt_ref.at[:, pl.ds(0, KEPT), :], virt_buf, local_sem.at[0])
    virt_copy.start()
    mine = pl.multiple_of(col * 128, 128)
    occ_copy = pltpu.make_async_copy(occ_ref, occ_buf.at[:, pl.ds(mine, 128)], local_sem.at[1])
    occ_copy.start()
    b_copies = [
        pltpu.make_async_copy(b_ref.at[p, :, pl.ds(0, KEPT), :], b_buf.at[p], b_sem.at[p]) for p in range(NP)
    ]
    for copy in b_copies:
        copy.start()

    rows_of = [wrap(row + o, NROW) for o in range(NROW)]
    ys_of = [wrap(y + o, NY) for o in range(NY)]
    cols_of = [wrap(col + o, NCOL) for o in range(NCOL)]
    deps_of = [wrap(dep + o, NDEP) for o in range(NDEP)]
    barrier = pltpu.get_barrier_semaphore()
    for o in range(1, NDEP):
        pl.semaphore_signal(barrier, inc=1, device_id=(row, col, deps_of[o]), device_id_type=MESH)
    for o in range(1, NROW):
        pl.semaphore_signal(barrier, inc=1, device_id=(rows_of[o], col, dep), device_id_type=MESH)
    for o in range(1, NCOL):
        pl.semaphore_signal(barrier, inc=1, device_id=(row, cols_of[o], dep), device_id_type=MESH)

    q = lax.broadcasted_iota(jnp.int32, (SIG, 128), 1)
    owner = 2 * ((q // 8) % 8) + q // 64
    column = owner * 32 + col * 8 + q % 8
    choose = jnp.where(lax.broadcasted_iota(jnp.int32, (SIG, 128), 0) == column, 1.0, 0.0).astype(BF16)
    virt_copy.wait()
    picked[...] = (
        jnp.dot(virt_buf[...].reshape(NB * KEPT, SIG), choose, preferred_element_type=F32)
        .astype(BF16)
        .reshape(NB, KEPT, 128)
    )

    first = row * NB
    for o in range(NROW):
        wanted = jnp.int32(0)
        for j in range(NB):
            t = target_ref[atom_ref[rows_of[o] * NB + j]] - first
            wanted += jnp.where((t >= 0) & (t < NB), t, 0)
        if o == 0:
            green_in[row] = picked[wanted]
        else:
            green_out[o] = picked[wanted]

    pl.semaphore_wait(barrier, NDEP + NROW + NCOL - 3)

    green_copies = []
    for o in (8, 9, 7, 10, 6, 11, 5, 12, 4, 13, 3, 14, 2, 15, 1):
        copy = pltpu.make_async_remote_copy(
            green_out.at[o], green_in.at[row], green_send.at[o], green_recv.at[row],
            device_id=(rows_of[o], col, dep), device_id_type=MESH,
        )
        copy.start()
        green_copies.append(copy)
    occ_copy.wait()
    occ_copies = []
    for o in range(1, NCOL):
        copy = pltpu.make_async_remote_copy(
            occ_buf.at[:, pl.ds(mine, 128)], occ_buf.at[:, pl.ds(mine, 128)], occ_send.at[o], occ_recv.at[col],
            device_id=(row, cols_of[o], dep), device_id_type=MESH,
        )
        copy.start()
        occ_copies.append(copy)

    def arrived(ref, send, recv):
        pltpu.make_async_copy(ref, ref, recv).wait()

    for o in range(1, NROW):
        arrived(green_in.at[rows_of[o]], None, green_recv.at[rows_of[o]])

    parts = []
    for j in range(NB):
        atom = atom_ref[row * NB + j]
        source = target_ref[atom] // NB
        kept = size_ref[atom] * screen_ref[atom]
        inside = lax.broadcasted_iota(jnp.int32, (KEPT, 128), 0) < kept
        parts.append(jnp.where(inside, green_in[source].astype(F32), 0.0).astype(BF16))
    rows_first = jnp.concatenate(parts, axis=0)
    eye = jnp.where(
        lax.broadcasted_iota(jnp.int32, (128, 128), 0) == lax.broadcasted_iota(jnp.int32, (128, 128), 1), 1.0, 0.0
    ).astype(BF16)
    green = lax.dot_general(eye, rows_first, (((1,), (1,)), ((), ())), preferred_element_type=F32).astype(BF16)

    pair_copies = []
    for g in range(GROUPS):
        for h in range(P_GROUP // 2):
            halves = []
            for k in range(2):
                p = g * P_GROUP + 2 * h + k
                b_copies[p].wait()
                block = b_buf[p].reshape(NB * KEPT, BS)
                halves.append(jnp.dot(green, block, preferred_element_type=F32).reshape(2, NY, 8, BS))
            y_buf[g, :, :, pl.ds(h * 16, 16), :] = jnp.concatenate(halves, axis=2).astype(BF16)
        copy = pltpu.make_async_remote_copy(
            y_buf.at[g, other], y_pair.at[g], pair_send.at[g], pair_recv.at[g],
            device_id=(row + 1 - 2 * core, col, dep), device_id_type=MESH,
        )
        copy.start()
        pair_copies.append(copy)

    y_copies = []
    for g in range(GROUPS):
        pair_copies[g].wait_recv()
        y_out[g] = (y_buf[g, core].astype(F32) + y_pair[g].astype(F32)).astype(BF16)
        for o in (4, 5, 3, 6, 2, 7, 1):
            copy = pltpu.make_async_remote_copy(
                y_out.at[g, ys_of[o]], y_in.at[g, y], y_send.at[g, o], y_recv.at[g, y],
                device_id=(2 * ys_of[o] + core, col, dep), device_id_type=MESH,
            )
            copy.start()
            y_copies.append(copy)
        y_in[g, y] = y_out[g, y]

    for o in range(1, NCOL):
        piece = occ_buf.at[:, pl.ds(pl.multiple_of(cols_of[o] * 128, 128), 128)]
        arrived(piece, None, occ_recv.at[cols_of[o]])
    occ_kept = lax.broadcasted_iota(jnp.int32, (BS, SIG), 0) < nu_ref[0]
    occ = jnp.where(occ_kept, occ_buf[...].astype(F32), 0.0).astype(BF16)

    for g in range(GROUPS):
        for o in range(1, NY):
            arrived(y_in.at[g, ys_of[o]], None, y_recv.at[g, ys_of[o]])
        total = y_in[g, 0].astype(F32)
        for k in range(1, NY):
            total += y_in[g, k].astype(F32)
        w = jnp.dot(total.astype(BF16), occ, preferred_element_type=F32)
        for k in range(P_GROUP):
            p = g * P_GROUP + k
            mine_w = w[k * 8 : (k + 1) * 8]
            w_out[p] = jnp.concatenate([mine_w[:, :256], mine_w[:, 256:]], axis=0).astype(BF16)

            @pl.when(dep != p)
            def _():
                pltpu.make_async_remote_copy(
                    w_out.at[p], w_in.at[dep], w_send.at[p], w_recv.at[dep],
                    device_id=(row, col, p), device_id_type=MESH,
                ).start()

    w_in[dep] = w_out[dep]
    for o in range(1, NDEP):
        arrived(w_in.at[deps_of[o]], None, w_recv.at[deps_of[o]])
    result = w_in[0].astype(F32)
    for k in range(1, NDEP):
        result += w_in[k].astype(F32)
    for c in range(NCOL):
        x_out[c] = result[(c // 2) * 8 : (c // 2) * 8 + 8, (c % 2) * 128 : (c % 2) * 128 + 128]
    x_copies = []
    for o in range(1, NCOL):
        copy = pltpu.make_async_remote_copy(
            x_out.at[cols_of[o]], out_ref.at[col], x_send.at[o], x_recv.at[col],
            device_id=(row, cols_of[o], dep), device_id_type=MESH,
        )
        copy.start()
        x_copies.append(copy)
    out_ref[col] = x_out[col]

    for copy in green_copies + occ_copies + pair_copies + y_copies:
        copy.wait_send()
    for o in range(1, NDEP):
        d = deps_of[o]
        pltpu.make_async_copy(w_out.at[d], w_out.at[d], w_send.at[d]).wait()
    for copy in x_copies:
        copy.wait_send()
    for o in range(1, NCOL):
        arrived(out_ref.at[cols_of[o]], None, x_recv.at[cols_of[o]])


def body(b_tensor, occ_green, virt_green, mu_atom, mu_target, mu_sizes, nu_sizes, screen):
    smem = pl.BlockSpec(memory_space=pltpu.SMEM)
    hbm = pl.BlockSpec(memory_space=pl.ANY)
    dma = pltpu.SemaphoreType.DMA
    out = pl.pallas_call(
        kernel,
        name="contract",
        out_shape=jax.ShapeDtypeStruct((NCOL, 8, 128), F32),
        in_specs=[smem] * 5 + [hbm] * 3,
        out_specs=pl.BlockSpec(memory_space=pltpu.VMEM),
        scratch_shapes=[
            pltpu.VMEM((NP, NB, KEPT, BS), BF16),
            pltpu.VMEM((NB, KEPT, SIG), BF16),
            pltpu.VMEM((BS, SIG), BF16),
            pltpu.VMEM((NB, KEPT, 128), BF16),
            pltpu.VMEM((NROW, KEPT, 128), BF16),
            pltpu.VMEM((NROW, KEPT, 128), BF16),
            pltpu.VMEM((GROUPS, 2, NY, ROWS_GROUP, BS), BF16),
            pltpu.VMEM((GROUPS, NY, ROWS_GROUP, BS), BF16),
            pltpu.VMEM((GROUPS, NY, ROWS_GROUP, BS), BF16),
            pltpu.VMEM((GROUPS, NY, ROWS_GROUP, BS), BF16),
            pltpu.VMEM((NP, 16, 256), BF16),
            pltpu.VMEM((NDEP, 16, 256), BF16),
            pltpu.VMEM((NCOL, 8, 128), F32),
            dma((NP,)),
            dma((2,)),
            dma((NROW,)),
            dma((NROW,)),
            dma((NCOL,)),
            dma((NCOL,)),
            dma((GROUPS,)),
            dma((GROUPS,)),
            dma((GROUPS, NY)),
            dma((GROUPS, NY)),
            dma((NP,)),
            dma((NDEP,)),
            dma((NCOL,)),
            dma((NCOL,)),
        ],
        compiler_params=pltpu.CompilerParams(
            collective_id=0, has_side_effects=True, vmem_limit_bytes=56 * 2**20
        ),
        cost_estimate=pl.CostEstimate(flops=1700000000, bytes_accessed=10000000, transcendentals=0),
    )(
        mu_atom,
        mu_target,
        mu_sizes,
        nu_sizes,
        screen.reshape(screen.shape[0]),
        b_tensor.reshape(NP, NB, BS, BS),
        virt_green.reshape(NB, BS, SIG),
        occ_green,
    )
    return out.reshape(SIG // NROW, 1, 128)


def solution(mesh):
    placed = (
        P(None, "row", "dep"),
        P("dep", "col"),
        P("row", None),
        P(),
        P(),
        P(),
        P("dep"),
        P(None, "dep"),
    )
    return jax.shard_map(
        body, mesh=mesh, in_specs=placed, out_specs=P("row", "dep", "col"), check_vma=False
    )
```

```python
import functools

import jax
import jax.numpy as jnp
from jax import lax
from jax.experimental import pallas as pl
from jax.experimental.pallas import tpu as pltpu
from jax.sharding import PartitionSpec as P

MESH = pl.DeviceIdType.MESH
BF16 = jnp.bfloat16
F32 = jnp.float32

BS = 256
NB = 6
KEPT = 208
NROW, NCOL, NDEP = 16, 4, 12
NY = NROW // 2
NP = 12
SIG = 512
GROUPS = 3
P_GROUP = NP // GROUPS
ROWS_GROUP = P_GROUP * 8


def wrap(value, size):
    return jnp.where(value >= size, value - size, value)


def kernel(
    atom_ref,
    target_ref,
    size_ref,
    nu_ref,
    screen_ref,
    b_ref,
    virt_ref,
    occ_ref,
    out_ref,
    b_buf,
    virt_buf,
    occ_buf,
    picked,
    green_out,
    green_in,
    y_buf,
    y_pair,
    y_out,
    y_in,
    w_out,
    w_in,
    x_out,
    b_sem,
    local_sem,
    green_send,
    green_recv,
    occ_send,
    occ_recv,
    pair_send,
    pair_recv,
    y_send,
    y_recv,
    w_send,
    w_recv,
    x_send,
    x_recv,
):
    row, col, dep = lax.axis_index("row"), lax.axis_index("col"), lax.axis_index("dep")
    core = lax.rem(row, 2)
    y = lax.div(row, 2)
    other = 1 - core

    virt_copy = pltpu.make_async_copy(virt_ref.at[:, pl.ds(0, KEPT), :], virt_buf, local_sem.at[0])
    virt_copy.start()
    mine = pl.multiple_of(col * 128, 128)
    occ_copy = pltpu.make_async_copy(occ_ref, occ_buf.at[:, pl.ds(mine, 128)], local_sem.at[1])
    occ_copy.start()
    b_copies = [
        pltpu.make_async_copy(b_ref.at[p, :, pl.ds(0, KEPT), :], b_buf.at[p], b_sem.at[p]) for p in range(NP)
    ]

    rows_of = [wrap(row + o, NROW) for o in range(NROW)]
    ys_of = [wrap(y + o, NY) for o in range(NY)]
    cols_of = [wrap(col + o, NCOL) for o in range(NCOL)]
    deps_of = [wrap(dep + o, NDEP) for o in range(NDEP)]
    barrier = pltpu.get_barrier_semaphore()
    for o in range(1, NDEP):
        pl.semaphore_signal(barrier, inc=1, device_id=(row, col, deps_of[o]), device_id_type=MESH)
    for o in range(1, NROW):
        pl.semaphore_signal(barrier, inc=1, device_id=(rows_of[o], col, dep), device_id_type=MESH)
    for o in range(1, NCOL):
        pl.semaphore_signal(barrier, inc=1, device_id=(row, cols_of[o], dep), device_id_type=MESH)

    with jax.named_scope("pick"):
        q = lax.broadcasted_iota(jnp.int32, (SIG, 128), 1)
        owner = 2 * ((q // 8) % 8) + q // 64
        column = owner * 32 + col * 8 + q % 8
        choose = jnp.where(lax.broadcasted_iota(jnp.int32, (SIG, 128), 0) == column, 1.0, 0.0).astype(BF16)
        virt_copy.wait()
        for copy in b_copies:
            copy.start()
        picked[...] = (
            jnp.dot(virt_buf[...].reshape(NB * KEPT, SIG), choose, preferred_element_type=F32)
            .astype(BF16)
            .reshape(NB, KEPT, 128)
        )

        first = row * NB
        for o in range(NROW):
            wanted = jnp.int32(0)
            for j in range(NB):
                t = target_ref[atom_ref[rows_of[o] * NB + j]] - first
                wanted += jnp.where((t >= 0) & (t < NB), t, 0)
            if o == 0:
                green_in[row] = picked[wanted]
            else:
                green_out[o] = picked[wanted]

    with jax.named_scope("barrier"):
        pl.semaphore_wait(barrier, NDEP + NROW + NCOL - 3)

    with jax.named_scope("green_send"):
        green_copies = []
        for o in (8, 9, 7, 10, 6, 11, 5, 12, 4, 13, 3, 14, 2, 15, 1):
            copy = pltpu.make_async_remote_copy(
                green_out.at[o], green_in.at[row], green_send.at[o], green_recv.at[row],
                device_id=(rows_of[o], col, dep), device_id_type=MESH,
            )
            copy.start()
            green_copies.append(copy)
        occ_copy.wait()
        occ_copies = []
        for o in range(1, NCOL):
            copy = pltpu.make_async_remote_copy(
                occ_buf.at[:, pl.ds(mine, 128)], occ_buf.at[:, pl.ds(mine, 128)], occ_send.at[o], occ_recv.at[col],
                device_id=(row, cols_of[o], dep), device_id_type=MESH,
            )
            copy.start()
            occ_copies.append(copy)

    def arrived(ref, send, recv):
        pltpu.make_async_copy(ref, ref, recv).wait()

    with jax.named_scope("green_wait"):
        for o in range(1, NROW):
            arrived(green_in.at[rows_of[o]], None, green_recv.at[rows_of[o]])

    with jax.named_scope("green_mask"):
        parts = []
        for j in range(NB):
            atom = atom_ref[row * NB + j]
            source = target_ref[atom] // NB
            kept = size_ref[atom] * screen_ref[atom]
            inside = lax.broadcasted_iota(jnp.int32, (KEPT, 128), 0) < kept
            parts.append(jnp.where(inside, green_in[source].astype(F32), 0.0).astype(BF16))
        rows_first = jnp.concatenate(parts, axis=0)
        eye = jnp.where(
            lax.broadcasted_iota(jnp.int32, (128, 128), 0) == lax.broadcasted_iota(jnp.int32, (128, 128), 1), 1.0, 0.0
        ).astype(BF16)
        green = lax.dot_general(eye, rows_first, (((1,), (1,)), ((), ())), preferred_element_type=F32).astype(BF16)

    with jax.named_scope("y_dot"):
        pair_copies = []
        for g in range(GROUPS):
            for h in range(P_GROUP // 2):
                halves = []
                for k in range(2):
                    p = g * P_GROUP + 2 * h + k
                    b_copies[p].wait()
                    block = b_buf[p].reshape(NB * KEPT, BS)
                    halves.append(jnp.dot(green, block, preferred_element_type=F32).reshape(2, NY, 8, BS))
                y_buf[g, :, :, pl.ds(h * 16, 16), :] = jnp.concatenate(halves, axis=2).astype(BF16)
            copy = pltpu.make_async_remote_copy(
                y_buf.at[g, other], y_pair.at[g], pair_send.at[g], pair_recv.at[g],
                device_id=(row + 1 - 2 * core, col, dep), device_id_type=MESH,
            )
            copy.start()
            pair_copies.append(copy)

    with jax.named_scope("pair_sum"):
        y_copies = []
        for g in range(GROUPS):
            pair_copies[g].wait_recv()
            y_out[g] = (y_buf[g, core].astype(F32) + y_pair[g].astype(F32)).astype(BF16)
            for o in (4, 5, 3, 6, 2, 7, 1):
                copy = pltpu.make_async_remote_copy(
                    y_out.at[g, ys_of[o]], y_in.at[g, y], y_send.at[g, o], y_recv.at[g, y],
                    device_id=(2 * ys_of[o] + core, col, dep), device_id_type=MESH,
                )
                copy.start()
                y_copies.append(copy)
            y_in[g, y] = y_out[g, y]

    for o in range(1, NCOL):
        piece = occ_buf.at[:, pl.ds(pl.multiple_of(cols_of[o] * 128, 128), 128)]
        arrived(piece, None, occ_recv.at[cols_of[o]])
    occ_kept = lax.broadcasted_iota(jnp.int32, (BS, SIG), 0) < nu_ref[0]
    occ = jnp.where(occ_kept, occ_buf[...].astype(F32), 0.0).astype(BF16)

    with jax.named_scope("y_sum"):
        for g in range(GROUPS):
            for o in range(1, NY):
                arrived(y_in.at[g, ys_of[o]], None, y_recv.at[g, ys_of[o]])
            total = y_in[g, 0].astype(F32)
            for k in range(1, NY):
                total += y_in[g, k].astype(F32)
            w = jnp.dot(total.astype(BF16), occ, preferred_element_type=F32)
            for k in range(P_GROUP):
                p = g * P_GROUP + k
                mine_w = w[k * 8 : (k + 1) * 8]
                w_out[p] = jnp.concatenate([mine_w[:, :256], mine_w[:, 256:]], axis=0).astype(BF16)

                @pl.when(dep != p)
                def _():
                    pltpu.make_async_remote_copy(
                        w_out.at[p], w_in.at[dep], w_send.at[p], w_recv.at[dep],
                        device_id=(row, col, p), device_id_type=MESH,
                    ).start()

    with jax.named_scope("w_sum"):
        w_in[dep] = w_out[dep]
        for o in range(1, NDEP):
            arrived(w_in.at[deps_of[o]], None, w_recv.at[deps_of[o]])
        result = w_in[0].astype(F32)
        for k in range(1, NDEP):
            result += w_in[k].astype(F32)
        for c in range(NCOL):
            x_out[c] = result[(c // 2) * 8 : (c // 2) * 8 + 8, (c % 2) * 128 : (c % 2) * 128 + 128]
    with jax.named_scope("x_end"):
        x_copies = []
        for o in range(1, NCOL):
            copy = pltpu.make_async_remote_copy(
                x_out.at[cols_of[o]], out_ref.at[col], x_send.at[o], x_recv.at[col],
                device_id=(row, cols_of[o], dep), device_id_type=MESH,
            )
            copy.start()
            x_copies.append(copy)
        out_ref[col] = x_out[col]

        for copy in green_copies + occ_copies + pair_copies + y_copies:
            copy.wait_send()
        for o in range(1, NDEP):
            d = deps_of[o]
            pltpu.make_async_copy(w_out.at[d], w_out.at[d], w_send.at[d]).wait()
        for copy in x_copies:
            copy.wait_send()
        for o in range(1, NCOL):
            arrived(out_ref.at[cols_of[o]], None, x_recv.at[cols_of[o]])


def body(b_tensor, occ_green, virt_green, mu_atom, mu_target, mu_sizes, nu_sizes, screen):
    smem = pl.BlockSpec(memory_space=pltpu.SMEM)
    hbm = pl.BlockSpec(memory_space=pl.ANY)
    dma = pltpu.SemaphoreType.DMA
    out = pl.pallas_call(
        kernel,
        name="contract",
        out_shape=jax.ShapeDtypeStruct((NCOL, 8, 128), F32),
        in_specs=[smem] * 5 + [hbm] * 3,
        out_specs=pl.BlockSpec(memory_space=pltpu.VMEM),
        scratch_shapes=[
            pltpu.VMEM((NP, NB, KEPT, BS), BF16),
            pltpu.VMEM((NB, KEPT, SIG), BF16),
            pltpu.VMEM((BS, SIG), BF16),
            pltpu.VMEM((NB, KEPT, 128), BF16),
            pltpu.VMEM((NROW, KEPT, 128), BF16),
            pltpu.VMEM((NROW, KEPT, 128), BF16),
            pltpu.VMEM((GROUPS, 2, NY, ROWS_GROUP, BS), BF16),
            pltpu.VMEM((GROUPS, NY, ROWS_GROUP, BS), BF16),
            pltpu.VMEM((GROUPS, NY, ROWS_GROUP, BS), BF16),
            pltpu.VMEM((GROUPS, NY, ROWS_GROUP, BS), BF16),
            pltpu.VMEM((NP, 16, 256), BF16),
            pltpu.VMEM((NDEP, 16, 256), BF16),
            pltpu.VMEM((NCOL, 8, 128), F32),
            dma((NP,)),
            dma((2,)),
            dma((NROW,)),
            dma((NROW,)),
            dma((NCOL,)),
            dma((NCOL,)),
            dma((GROUPS,)),
            dma((GROUPS,)),
            dma((GROUPS, NY)),
            dma((GROUPS, NY)),
            dma((NP,)),
            dma((NDEP,)),
            dma((NCOL,)),
            dma((NCOL,)),
        ],
        compiler_params=pltpu.CompilerParams(
            collective_id=0, has_side_effects=True, vmem_limit_bytes=56 * 2**20
        ),
        cost_estimate=pl.CostEstimate(flops=1700000000, bytes_accessed=10000000, transcendentals=0),
    )(
        mu_atom,
        mu_target,
        mu_sizes,
        nu_sizes,
        screen.reshape(screen.shape[0]),
        b_tensor.reshape(NP, NB, BS, BS),
        virt_green.reshape(NB, BS, SIG),
        occ_green,
    )
    return out.reshape(SIG // NROW, 1, 128)


def solution(mesh):
    placed = (
        P(None, "row", "dep"),
        P("dep", "col"),
        P("row", None),
        P(),
        P(),
        P(),
        P("dep"),
        P(None, "dep"),
    )
    return jax.shard_map(
        body, mesh=mesh, in_specs=placed, out_specs=P("row", "dep", "col"), check_vma=False
    )
```

```python
import jax
import jax.numpy as jnp
from jax import lax
from jax.experimental import pallas as pl
from jax.experimental.pallas import tpu as pltpu
from jax.sharding import PartitionSpec as P

MESH = pl.DeviceIdType.MESH
BF16 = jnp.bfloat16
F32 = jnp.float32

BS = 256
NB = 6
KEPT = 208
SHARE = 64
TAIL = KEPT - 3 * SHARE
NROW, NCOL, NDEP = 16, 4, 12
NY = NROW // 2
NP = 12
SIG = 512
LAG = 2
GROUPS = 6
P_GROUP = NP // GROUPS
ROWS_GROUP = P_GROUP * 8


def wrap(value, size):
    return jnp.where(value >= size, value - size, value)


def arrived(ref, sem):
    pltpu.make_async_copy(ref, ref, sem).wait()


def kernel(
    atom_ref,
    target_ref,
    size_ref,
    nu_ref,
    screen_ref,
    b_ref,
    virt_ref,
    occ_ref,
    out_ref,
    b_buf,
    virt_buf,
    occ_buf,
    occ_kept,
    picked,
    green_out,
    green_in,
    green_all,
    y_buf,
    y_pair,
    y_out,
    y_in,
    w_out,
    w_in,
    b_sem,
    local_sem,
    green_send,
    green_recv,
    share_send,
    share_recv,
    occ_send,
    occ_recv,
    pair_send,
    pair_recv,
    y_send,
    y_recv,
    w_send,
    w_recv,
):
    row, col, dep = lax.axis_index("row"), lax.axis_index("col"), lax.axis_index("dep")
    core = lax.rem(row, 2)
    y = lax.div(row, 2)
    other = 1 - core
    share = lax.rem(dep, 3)
    here = pl.ds(pl.multiple_of(share * SHARE, SHARE), SHARE)
    tail = pl.ds(3 * SHARE, TAIL)

    rows_of = [wrap(row + o, NROW) for o in range(NROW)]
    ys_of = [wrap(y + o, NY) for o in range(NY)]
    cols_of = [wrap(col + o, NCOL) for o in range(NCOL)]
    deps_of = [wrap(dep + o, NDEP) for o in range(NDEP)]
    virt_copies = [
        pltpu.make_async_copy(virt_ref.at[:, here, :], virt_buf.at[:, pl.ds(0, SHARE), :], local_sem.at[0]),
        pltpu.make_async_copy(virt_ref.at[:, tail, :], virt_buf.at[:, pl.ds(SHARE, TAIL), :], local_sem.at[1]),
    ]
    for copy in virt_copies:
        copy.start()
    barrier = pltpu.get_barrier_semaphore()
    for o in (6, 5, 7, 4, 8, 3, 9, 2, 10, 1, 11):
        pl.semaphore_signal(barrier, inc=1, device_id=(row, col, deps_of[o]), device_id_type=MESH)
    for o in range(1, NROW):
        pl.semaphore_signal(barrier, inc=1, device_id=(rows_of[o], col, dep), device_id_type=MESH)
    for o in range(1, NCOL):
        pl.semaphore_signal(barrier, inc=1, device_id=(row, cols_of[o], dep), device_id_type=MESH)

    first = row * NB
    wanted = []
    for o in range(NROW):
        found = jnp.int32(0)
        for j in range(NB):
            t = target_ref[atom_ref[rows_of[o] * NB + j]] - first
            found += jnp.where((t >= 0) & (t < NB), t, 0)
        wanted.append(found)

    q = lax.broadcasted_iota(jnp.int32, (1, 128), 1)
    column = (2 * ((q >> 3) & 7) + (q >> 6)) * 32 + col * 8 + (q & 7)
    choose = jnp.where(lax.broadcasted_iota(jnp.int32, (SIG, 128), 0) == column, 1.0, 0.0).astype(BF16)
    for copy in virt_copies:
        copy.wait()
    picked[...] = (
        jnp.dot(virt_buf[...].reshape(NB * (SHARE + TAIL), SIG), choose, preferred_element_type=F32)
        .astype(BF16)
        .reshape(NB, SHARE + TAIL, 128)
    )
    for o in range(NROW):
        if o == 0:
            green_in[row] = picked[wanted[o]]
        else:
            green_out[o] = picked[wanted[o]]

    pl.semaphore_wait(barrier, NDEP + NROW + NCOL - 3)
    sent = []

    for o in (8, 9, 7, 10, 6, 11, 5, 12, 4, 13, 3, 14, 2, 15, 1):
        copy = pltpu.make_async_remote_copy(
            green_out.at[o], green_in.at[row], green_send.at[0], green_recv.at[0],
            device_id=(rows_of[o], col, dep), device_id_type=MESH,
        )
        copy.start()
    mine = pl.multiple_of(col * 128, 128)
    occ_copy = pltpu.make_async_copy(occ_ref, occ_buf.at[:, pl.ds(mine, 128)], local_sem.at[2])
    occ_copy.start()
    b_copies = [
        pltpu.make_async_copy(b_ref.at[p, :, pl.ds(0, KEPT), :], b_buf.at[p], b_sem.at[p]) for p in range(NP)
    ]

    for copy in b_copies:
        copy.start()
    occ_copy.wait()
    for o in range(1, NCOL):
        copy = pltpu.make_async_remote_copy(
            occ_buf.at[:, pl.ds(mine, 128)], occ_buf.at[:, pl.ds(mine, 128)], occ_send.at[o], occ_recv.at[col],
            device_id=(row, cols_of[o], dep), device_id_type=MESH,
        )
        copy.start()
        sent.append(copy)

    arrived(green_out.at[pl.ds(1, NROW - 1)], green_recv.at[0])

    for j in range(NB):
        source = target_ref[atom_ref[row * NB + j]] // NB
        block = green_in[source]
        green_all[j, here, :] = block[:SHARE]
        green_all[j, tail, :] = block[SHARE:]
    for o in (1, NDEP - 1):
        copy = pltpu.make_async_remote_copy(
            green_all.at[:, here, :], green_all.at[:, here, :], share_send.at[o // 11], share_recv.at[o // 11],
            device_id=(row, col, deps_of[o]), device_id_type=MESH,
        )
        copy.start()
        sent.append(copy)
    for o in range(1, NCOL):
        piece = occ_buf.at[:, pl.ds(pl.multiple_of(cols_of[o] * 128, 128), 128)]
        arrived(piece, occ_recv.at[cols_of[o]])
    inside = lax.broadcasted_iota(jnp.int32, (BS, SIG), 0) < nu_ref[0]
    occ_kept[...] = jnp.where(inside, occ_buf[...].astype(F32), 0.0).astype(BF16)
    before = pl.ds(pl.multiple_of(lax.rem(share + 2, 3) * SHARE, SHARE), SHARE)
    after = pl.ds(pl.multiple_of(lax.rem(share + 1, 3) * SHARE, SHARE), SHARE)
    arrived(green_all.at[:, before, :], share_recv.at[0])
    arrived(green_all.at[:, after, :], share_recv.at[1])

    parts = []
    for j in range(NB):
        atom = atom_ref[row * NB + j]
        kept = size_ref[atom] * screen_ref[atom]
        inside = lax.broadcasted_iota(jnp.int32, (KEPT, 128), 0) < kept
        parts.append(jnp.where(inside, green_all[j].astype(F32), 0.0).astype(BF16))
    rows_first = jnp.concatenate(parts, axis=0)
    green = rows_first.T

    pair_copies = []

    def contract_first(g):
        for h in range(P_GROUP // 2):
            halves = []
            for k in range(2):
                p = g * P_GROUP + 2 * h + k
                b_copies[p].wait()
                block = b_buf[p].reshape(NB * KEPT, BS)
                halves.append(jnp.dot(green, block, preferred_element_type=F32).reshape(2, NY, 8, BS))
            y_buf[g, :, :, pl.ds(h * 16, 16), :] = jnp.concatenate(halves, axis=2).astype(BF16)
        copy = pltpu.make_async_remote_copy(
            y_buf.at[g, other], y_pair.at[g], pair_send.at[g], pair_recv.at[g],
            device_id=(row + 1 - 2 * core, col, dep), device_id_type=MESH,
        )
        copy.start()
        pair_copies.append(copy)
        sent.append(copy)

    def send_over_y(g):
        pair_copies[g].wait_recv()
        y_out[g] = (y_buf[g, core].astype(F32) + y_pair[g].astype(F32)).astype(BF16)
        for o in (4, 5, 3, 6, 2, 7, 1):
            copy = pltpu.make_async_remote_copy(
                y_out.at[g, ys_of[o]], y_in.at[g, y], y_send.at[0], y_recv.at[g],
                device_id=(2 * ys_of[o] + core, col, dep), device_id_type=MESH,
            )
            copy.start()
        y_in[g, y] = y_out[g, y]

    for g in range(GROUPS):
        contract_first(g)
        if g >= LAG:
            send_over_y(g - LAG)
    for g in range(GROUPS - LAG, GROUPS):
        send_over_y(g)

    for g in range(GROUPS):
        arrived(y_out.at[g, pl.ds(1, NY - 1)], y_recv.at[g])
        total = y_in[g, 0].astype(F32)
        for k in range(1, NY):
            total += y_in[g, k].astype(F32)
        w = jnp.dot(total.astype(BF16), occ_kept[...], preferred_element_type=F32)
        for k in range(P_GROUP):
            p = g * P_GROUP + k
            for c in range(NCOL):
                w_out[p * NCOL + c] = w[k * 8 : (k + 1) * 8, c * 128 : (c + 1) * 128]
            for o in (2, 1, 3, 0):
                c = cols_of[o]

                def send():
                    pltpu.make_async_remote_copy(
                        w_out.at[p * NCOL + c], w_in.at[dep * NCOL + col], w_send.at[0], w_recv.at[0],
                        device_id=(row, c, p), device_id_type=MESH,
                    ).start()

                if o == 0:
                    pl.when(dep != p)(send)
                else:
                    send()

    w_in[dep * NCOL + col] = w_out[dep * NCOL + col]
    others = pl.ds(1, NDEP * NCOL - 1)
    arrived(w_in.at[others], w_recv.at[0])
    for c in range(NCOL):
        result = w_in[c]
        for k in range(1, NDEP):
            result += w_in[k * NCOL + c]
        out_ref[c] = result
    arrived(w_out.at[others], w_send.at[0])
    arrived(green_out.at[pl.ds(1, NROW - 1)], green_send.at[0])
    arrived(y_out.at[:, pl.ds(1, NY - 1)], y_send.at[0])
    for copy in sent:
        copy.wait_send()


def body(b_tensor, occ_green, virt_green, mu_atom, mu_target, mu_sizes, nu_sizes, screen):
    smem = pl.BlockSpec(memory_space=pltpu.SMEM)
    hbm = pl.BlockSpec(memory_space=pl.ANY)
    dma = pltpu.SemaphoreType.DMA
    out = pl.pallas_call(
        kernel,
        name="contract",
        out_shape=jax.ShapeDtypeStruct((NCOL, 8, 128), F32),
        in_specs=[smem] * 5 + [hbm] * 3,
        out_specs=pl.BlockSpec(memory_space=pltpu.VMEM),
        scratch_shapes=[
            pltpu.VMEM((NP, NB, KEPT, BS), BF16),
            pltpu.VMEM((NB, SHARE + TAIL, SIG), BF16),
            pltpu.VMEM((BS, SIG), BF16),
            pltpu.VMEM((BS, SIG), BF16),
            pltpu.VMEM((NB, SHARE + TAIL, 128), BF16),
            pltpu.VMEM((NROW, SHARE + TAIL, 128), BF16),
            pltpu.VMEM((NROW, SHARE + TAIL, 128), BF16),
            pltpu.VMEM((NB, KEPT, 128), BF16),
            pltpu.VMEM((GROUPS, 2, NY, ROWS_GROUP, BS), BF16),
            pltpu.VMEM((GROUPS, NY, ROWS_GROUP, BS), BF16),
            pltpu.VMEM((GROUPS, NY, ROWS_GROUP, BS), BF16),
            pltpu.VMEM((GROUPS, NY, ROWS_GROUP, BS), BF16),
            pltpu.VMEM((NP * NCOL, 8, 128), F32),
            pltpu.VMEM((NDEP * NCOL, 8, 128), F32),
            dma((NP,)),
            dma((3,)),
            dma((1,)),
            dma((1,)),
            dma((2,)),
            dma((2,)),
            dma((NCOL,)),
            dma((NCOL,)),
            dma((GROUPS,)),
            dma((GROUPS,)),
            dma((1,)),
            dma((GROUPS,)),
            dma((1,)),
            dma((1,)),
        ],
        compiler_params=pltpu.CompilerParams(
            collective_id=0, has_side_effects=True, vmem_limit_bytes=56 * 2**20
        ),
        cost_estimate=pl.CostEstimate(flops=1700000000, bytes_accessed=10000000, transcendentals=0),
    )(
        mu_atom,
        mu_target,
        mu_sizes,
        nu_sizes,
        screen.reshape(screen.shape[0]),
        b_tensor.reshape(NP, NB, BS, BS),
        virt_green.reshape(NB, BS, SIG),
        occ_green,
    )
    return out.reshape(SIG // NROW, 1, 128)


def solution(mesh):
    placed = (
        P(None, "row", "dep"),
        P("dep", "col"),
        P("row", None),
        P(),
        P(),
        P(),
        P("dep"),
        P(None, "dep"),
    )
    return jax.shard_map(
        body, mesh=mesh, in_specs=placed, out_specs=P("row", "dep", "col"), check_vma=False
    )
```

```python
import jax
import jax.numpy as jnp
from jax import lax
from jax.experimental import pallas as pl
from jax.experimental.pallas import tpu as pltpu
from jax.sharding import PartitionSpec as P

MESH = pl.DeviceIdType.MESH
BF16 = jnp.bfloat16
F32 = jnp.float32

BS = 256
NB = 6
KEPT = 208
SHARE = 64
TAIL = KEPT - 3 * SHARE
NROW, NCOL, NDEP = 16, 4, 12
NY = NROW // 2
NP = 12
SIG = 512
PAIRS = NP // 4
FAR_FIRST = (8, 9, 7, 10, 6, 11, 5, 12, 4, 13, 3, 14, 2, 15, 1)


def wrap(value, size):
    return jnp.where(value >= size, value - size, value)


def arrived(ref, sem):
    pltpu.make_async_copy(ref, ref, sem).wait()


def kernel(
    atom_ref,
    target_ref,
    size_ref,
    nu_ref,
    screen_ref,
    b_ref,
    virt_ref,
    occ_ref,
    out_ref,
    b_buf,
    virt_buf,
    occ_buf,
    occ_kept,
    picked,
    green_out,
    green_in,
    green_all,
    green_ref,
    y_buf,
    y_pair,
    y_out,
    y_in,
    w_out,
    w_in,
    b_sem,
    local_sem,
    green_send,
    green_recv,
    share_send,
    share_recv,
    occ_send,
    occ_recv,
    pair_send,
    pair_recv,
    y_send,
    y_recv,
    w_send,
    w_recv,
):
    row, col, dep = lax.axis_index("row"), lax.axis_index("col"), lax.axis_index("dep")
    core = lax.rem(row, 2)
    y = lax.div(row, 2)
    other = 1 - core
    parity = lax.div(col, 2)
    share = lax.rem(dep, 3)
    here = pl.ds(pl.multiple_of(share * SHARE, SHARE), SHARE)
    tail = pl.ds(3 * SHARE, TAIL)

    rows_of = [wrap(row + o, NROW) for o in range(NROW)]
    ys_of = [wrap(y + o, NY) for o in range(NY)]
    cols_of = [wrap(col + o, NCOL) for o in range(NCOL)]
    deps_of = [wrap(dep + o, NDEP) for o in range(NDEP)]
    virt_copies = [
        pltpu.make_async_copy(virt_ref.at[:, here, :], virt_buf.at[:, pl.ds(0, SHARE), :], local_sem.at[0]),
        pltpu.make_async_copy(virt_ref.at[:, tail, :], virt_buf.at[:, pl.ds(SHARE, TAIL), :], local_sem.at[1]),
    ]
    for copy in virt_copies:
        copy.start()
    barrier = pltpu.get_barrier_semaphore()
    for o in (6, 5, 7, 4, 8, 3, 9, 2, 10, 1, 11):
        pl.semaphore_signal(barrier, inc=1, device_id=(row, col, deps_of[o]), device_id_type=MESH)
    for o in FAR_FIRST:
        pl.semaphore_signal(barrier, inc=1, device_id=(rows_of[o], col, dep), device_id_type=MESH)
    for o in range(1, NCOL):
        pl.semaphore_signal(barrier, inc=1, device_id=(row, cols_of[o], dep), device_id_type=MESH)

    q = lax.broadcasted_iota(jnp.int32, (1, 128), 1)
    column = (2 * (q >> 4) + parity) * 32 + lax.rem(col, 2) * 16 + (q & 15)
    choose = jnp.where(lax.broadcasted_iota(jnp.int32, (SIG, 128), 0) == column, 1.0, 0.0).astype(BF16)
    for copy in virt_copies:
        copy.wait()
    picked[...] = (
        jnp.dot(virt_buf[...].reshape(NB * (SHARE + TAIL), SIG), choose, preferred_element_type=F32)
        .astype(BF16)
        .reshape(NB, SHARE + TAIL, 128)
    )

    first = row * NB

    @pl.loop(0, NROW)
    def _(r):
        found = jnp.int32(0)
        for j in range(NB):
            t = target_ref[atom_ref[r * NB + j]] - first
            found += jnp.where((t >= 0) & (t < NB), t, 0)
        green_out[r] = picked[found]

    pl.semaphore_wait(barrier, NDEP + NROW + NCOL - 3)
    sent = []

    @pl.loop(0, NROW - 1)
    def _(i):
        o = jnp.where(lax.rem(i, 2) == 1, NY + lax.div(i + 1, 2), NY - lax.div(i, 2))
        to = wrap(row + o, NROW)
        pltpu.make_async_remote_copy(
            green_out.at[to], green_in.at[row], green_send.at[0], green_recv.at[0],
            device_id=(to, col, dep), device_id_type=MESH,
        ).start()

    green_in[row] = green_out[row]
    mine = pl.multiple_of(col * 128, 128)
    occ_copy = pltpu.make_async_copy(occ_ref, occ_buf.at[:, pl.ds(mine, 128)], local_sem.at[2])
    occ_copy.start()

    @pl.loop(0, NP)
    def _(p):
        pltpu.make_async_copy(b_ref.at[p, :, pl.ds(0, KEPT), :], b_buf.at[p], b_sem.at[p]).start()

    arrived(green_out.at[pl.ds(1, NROW - 1)], green_recv.at[0])

    for j in range(NB):
        source = target_ref[atom_ref[row * NB + j]] // NB
        block = green_in[source]
        green_all[j, here, :] = block[:SHARE]
        green_all[j, tail, :] = block[SHARE:]
    for o in (1, NDEP - 1):
        copy = pltpu.make_async_remote_copy(
            green_all.at[:, here, :], green_all.at[:, here, :], share_send.at[o // 11], share_recv.at[o // 11],
            device_id=(row, col, deps_of[o]), device_id_type=MESH,
        )
        copy.start()
        sent.append(copy)
    occ_copy.wait()
    for o in range(1, NCOL):
        copy = pltpu.make_async_remote_copy(
            occ_buf.at[:, pl.ds(mine, 128)], occ_buf.at[:, pl.ds(mine, 128)], occ_send.at[o], occ_recv.at[col],
            device_id=(row, cols_of[o], dep), device_id_type=MESH,
        )
        copy.start()
        sent.append(copy)
    before = pl.ds(pl.multiple_of(lax.rem(share + 2, 3) * SHARE, SHARE), SHARE)
    after = pl.ds(pl.multiple_of(lax.rem(share + 1, 3) * SHARE, SHARE), SHARE)
    arrived(green_all.at[:, before, :], share_recv.at[0])
    arrived(green_all.at[:, after, :], share_recv.at[1])

    parts = []
    for j in range(NB):
        atom = atom_ref[row * NB + j]
        kept = size_ref[atom] * screen_ref[atom]
        inside = lax.broadcasted_iota(jnp.int32, (KEPT, 128), 0) < kept
        parts.append(jnp.where(inside, green_all[j].astype(F32), 0.0).astype(BF16))
    rows_first = jnp.concatenate(parts, axis=0)
    green_ref[...] = rows_first.T


    def pair_copy(m):
        return pltpu.make_async_remote_copy(
            y_buf.at[2 * m + other], y_pair.at[m], pair_send.at[m], pair_recv.at[m],
            device_id=(row + 1 - 2 * core, col, dep), device_id_type=MESH,
        )

    def contract_first(m, owner):
        @pl.loop(0, 2)
        def _(k):
            p = 4 * m + 2 * owner + k
            arrived(b_buf.at[p], b_sem.at[p])
            block = b_buf[p].reshape(NB * KEPT, BS)
            product = jnp.dot(green_ref[...], block, preferred_element_type=F32).astype(BF16).reshape(NY, 16, BS)
            y_buf[2 * m + owner, :, pl.ds(pl.multiple_of(k * 16, 16), 16), :] = product

    @pl.loop(0, PAIRS)
    def _(m):
        @pl.loop(0, 2)
        def _(t):
            contract_first(m, jnp.where(t == 0, other, core))
            pl.when(t == 0)(lambda: pair_copy(m).start())
        pair_copy(m).wait_recv()
        y_out[m] = (y_buf[2 * m + core].astype(F32) + y_pair[m].astype(F32)).astype(BF16)
        @pl.loop(0, NY - 1)
        def _(i):
            half = NY // 2
            o = jnp.where(lax.rem(i, 2) == 1, half + lax.div(i + 1, 2), half - lax.div(i, 2))
            to = wrap(y + o, NY)
            pltpu.make_async_remote_copy(
                y_out.at[m, to], y_in.at[m, y], y_send.at[0], y_recv.at[m],
                device_id=(2 * to + core, col, dep), device_id_type=MESH,
            ).start()

        y_in[m, y] = y_out[m, y]

    for o in range(1, NCOL):
        piece = occ_buf.at[:, pl.ds(pl.multiple_of(cols_of[o] * 128, 128), 128)]
        arrived(piece, occ_recv.at[cols_of[o]])
    inside = lax.broadcasted_iota(jnp.int32, (BS, SIG), 0) < nu_ref[0]
    occ_kept[...] = jnp.where(inside, occ_buf[...].astype(F32), 0.0).astype(BF16)

    own = (core == parity) & (lax.rem(lax.div(dep, 2), 2) == core)
    @pl.loop(0, PAIRS)
    def _(m):
        arrived(y_out.at[m, pl.ds(1, NY - 1)], y_recv.at[m])
        total = y_in[m, 0].astype(F32)
        for k in range(1, NY):
            total += y_in[m, k].astype(F32)
        w = jnp.dot(total.astype(BF16), occ_kept[...], preferred_element_type=F32).astype(BF16)
        for k in range(2):
            for c in range(NCOL):
                w_out[(2 * m + k) * NCOL + c] = w[k * 16 : (k + 1) * 16, c * 128 : (c + 1) * 128]
        @pl.loop(0, 2 * NCOL)
        def _(i):
            p = 4 * m + 2 * core + lax.div(i, NCOL)
            c = lax.rem(i, NCOL)
            slot = 2 * m * NCOL + i
            same = own & (dep == p) & (col == c)

            @pl.when(jnp.logical_not(same))
            def _():
                pltpu.make_async_remote_copy(
                    w_out.at[slot], w_in.at[dep * 2 + lax.rem(col, 2)], w_send.at[0], w_recv.at[0],
                    device_id=(2 * y + parity, c, p), device_id_type=MESH,
                ).start()

            @pl.when(same)
            def _():
                w_in[dep * 2 + lax.rem(col, 2)] = w_out[slot]

    @pl.when(own)
    def _():
        arrived(w_in.at[pl.ds(0, 2 * NDEP - 1)], w_recv.at[0])

    @pl.when(jnp.logical_not(own))
    def _():
        arrived(w_in, w_recv.at[0])

    for c in range(2):
        result = w_in[c].astype(F32)
        for k in range(1, NDEP):
            result += w_in[2 * k + c].astype(F32)
        out_ref[c] = result

    @pl.when(own)
    def _():
        arrived(w_out.at[pl.ds(0, 2 * NDEP - 1)], w_send.at[0])

    @pl.when(jnp.logical_not(own))
    def _():
        arrived(w_out, w_send.at[0])
    arrived(green_out.at[pl.ds(1, NROW - 1)], green_send.at[0])
    arrived(y_out.at[:, pl.ds(1, NY - 1)], y_send.at[0])
    for m in range(PAIRS):
        pair_copy(m).wait_send()
    for copy in sent:
        copy.wait_send()


def body(b_tensor, occ_green, virt_green, mu_atom, mu_target, mu_sizes, nu_sizes, screen):
    smem = pl.BlockSpec(memory_space=pltpu.SMEM)
    hbm = pl.BlockSpec(memory_space=pl.ANY)
    dma = pltpu.SemaphoreType.DMA
    out = pl.pallas_call(
        kernel,
        name="contract",
        out_shape=jax.ShapeDtypeStruct((2, 16, 128), F32),
        in_specs=[smem] * 5 + [hbm] * 3,
        out_specs=pl.BlockSpec(memory_space=pltpu.VMEM),
        scratch_shapes=[
            pltpu.VMEM((NP, NB, KEPT, BS), BF16),
            pltpu.VMEM((NB, SHARE + TAIL, SIG), BF16),
            pltpu.VMEM((BS, SIG), BF16),
            pltpu.VMEM((BS, SIG), BF16),
            pltpu.VMEM((NB, SHARE + TAIL, 128), BF16),
            pltpu.VMEM((NROW, SHARE + TAIL, 128), BF16),
            pltpu.VMEM((NROW, SHARE + TAIL, 128), BF16),
            pltpu.VMEM((NB, KEPT, 128), BF16),
            pltpu.VMEM((128, NB * KEPT), BF16),
            pltpu.VMEM((2 * PAIRS, NY, 32, BS), BF16),
            pltpu.VMEM((PAIRS, NY, 32, BS), BF16),
            pltpu.VMEM((PAIRS, NY, 32, BS), BF16),
            pltpu.VMEM((PAIRS, NY, 32, BS), BF16),
            pltpu.VMEM((2 * PAIRS * NCOL, 16, 128), BF16),
            pltpu.VMEM((2 * NDEP, 16, 128), BF16),
            dma((NP,)),
            dma((3,)),
            dma((1,)),
            dma((1,)),
            dma((2,)),
            dma((2,)),
            dma((NCOL,)),
            dma((NCOL,)),
            dma((PAIRS,)),
            dma((PAIRS,)),
            dma((1,)),
            dma((PAIRS,)),
            dma((1,)),
            dma((1,)),
        ],
        compiler_params=pltpu.CompilerParams(
            collective_id=0, has_side_effects=True, vmem_limit_bytes=56 * 2**20
        ),
        cost_estimate=pl.CostEstimate(flops=1700000000, bytes_accessed=10000000, transcendentals=0),
    )(
        mu_atom,
        mu_target,
        mu_sizes,
        nu_sizes,
        screen.reshape(screen.shape[0]),
        b_tensor.reshape(NP, NB, BS, BS),
        virt_green.reshape(NB, BS, SIG),
        occ_green,
    )
    return out.reshape(SIG // NROW, 1, 128)


def solution(mesh):
    placed = (
        P(None, "row", "dep"),
        P("dep", "col"),
        P("row", None),
        P(),
        P(),
        P(),
        P("dep"),
        P(None, "dep"),
    )
    return jax.shard_map(
        body, mesh=mesh, in_specs=placed, out_specs=P("row", "dep", "col"), check_vma=False
    )
```

```python
import jax
import jax.numpy as jnp
from jax import lax
from jax.experimental import pallas as pl
from jax.experimental.pallas import tpu as pltpu
from jax.sharding import PartitionSpec as P

MESH = pl.DeviceIdType.MESH
BF16 = jnp.bfloat16
F32 = jnp.float32

BS = 256
NB = 6
KEPT = 208
SHARE = 64
TAIL = KEPT - 3 * SHARE
NROW, NCOL, NDEP = 16, 4, 12
NY = NROW // 2
NP = 12
SIG = 512
STEPS = NP // 2
Y_ORDER = (0, 1, 2, 7, 3, 6, 5, 4)
FAR_FIRST = (8, 9, 7, 10, 6, 11, 5, 12, 4, 13, 3, 14, 2, 15, 1)


def wrap(value, size):
    return jnp.where(value >= size, value - size, value)


def arrived(ref, sem):
    pltpu.make_async_copy(ref, ref, sem).wait()


def kernel(
    atom_ref,
    target_ref,
    size_ref,
    nu_ref,
    screen_ref,
    b_ref,
    virt_ref,
    occ_ref,
    out_ref,
    b_buf,
    virt_buf,
    occ_buf,
    occ_kept,
    picked,
    green_out,
    green_in,
    green_all,
    green_ref,
    y_buf,
    y_pair,
    y_out,
    y_in,
    w_out,
    w_in,
    b_sem,
    local_sem,
    green_send,
    green_recv,
    share_send,
    share_recv,
    occ_send,
    occ_recv,
    pair_send,
    pair_recv,
    y_send,
    y_recv,
    w_send,
    w_recv,
):
    row, col, dep = lax.axis_index("row"), lax.axis_index("col"), lax.axis_index("dep")
    core = lax.rem(row, 2)
    y = lax.div(row, 2)
    other = 1 - core
    parity = lax.div(col, 2)
    share = lax.rem(dep, 3)
    here = pl.ds(pl.multiple_of(share * SHARE, SHARE), SHARE)
    tail = pl.ds(3 * SHARE, TAIL)

    rows_of = [wrap(row + o, NROW) for o in range(NROW)]
    ys_of = [wrap(y + o, NY) for o in range(NY)]
    cols_of = [wrap(col + o, NCOL) for o in range(NCOL)]
    deps_of = [wrap(dep + o, NDEP) for o in range(NDEP)]
    virt_copies = [
        pltpu.make_async_copy(virt_ref.at[:, here, :], virt_buf.at[:, pl.ds(0, SHARE), :], local_sem.at[0]),
        pltpu.make_async_copy(virt_ref.at[:, tail, :], virt_buf.at[:, pl.ds(SHARE, TAIL), :], local_sem.at[1]),
    ]
    for copy in virt_copies:
        copy.start()
    barrier = pltpu.get_barrier_semaphore()
    for o in (6, 5, 7, 4, 8, 3, 9, 2, 10, 1, 11):
        pl.semaphore_signal(barrier, inc=1, device_id=(row, col, deps_of[o]), device_id_type=MESH)
    for o in FAR_FIRST:
        pl.semaphore_signal(barrier, inc=1, device_id=(rows_of[o], col, dep), device_id_type=MESH)
    for o in range(1, NCOL):
        pl.semaphore_signal(barrier, inc=1, device_id=(row, cols_of[o], dep), device_id_type=MESH)

    q = lax.broadcasted_iota(jnp.int32, (1, 128), 1)
    column = (2 * (q >> 4) + parity) * 32 + lax.rem(col, 2) * 16 + (q & 15)
    choose = jnp.where(lax.broadcasted_iota(jnp.int32, (SIG, 128), 0) == column, 1.0, 0.0).astype(BF16)
    for copy in virt_copies:
        copy.wait()
    picked[...] = (
        jnp.dot(virt_buf[...].reshape(NB * (SHARE + TAIL), SIG), choose, preferred_element_type=F32)
        .astype(BF16)
        .reshape(NB, SHARE + TAIL, 128)
    )

    first = row * NB

    @pl.loop(0, NROW)
    def _(r):
        found = jnp.int32(0)
        for j in range(NB):
            t = target_ref[atom_ref[r * NB + j]] - first
            found += jnp.where((t >= 0) & (t < NB), t, 0)
        green_out[r] = picked[found]

    pl.semaphore_wait(barrier, NDEP + NROW + NCOL - 3)
    sent = []

    @pl.loop(0, NROW - 1)
    def _(i):
        o = jnp.where(lax.rem(i, 2) == 1, NY + lax.div(i + 1, 2), NY - lax.div(i, 2))
        to = wrap(row + o, NROW)
        pltpu.make_async_remote_copy(
            green_out.at[to], green_in.at[row], green_send.at[0], green_recv.at[0],
            device_id=(to, col, dep), device_id_type=MESH,
        ).start()

    green_in[row] = green_out[row]
    mine = pl.multiple_of(col * 128, 128)
    occ_copy = pltpu.make_async_copy(occ_ref, occ_buf.at[:, pl.ds(mine, 128)], local_sem.at[2])
    occ_copy.start()

    @pl.loop(0, NP)
    def _(p):
        pltpu.make_async_copy(b_ref.at[p, :, pl.ds(0, KEPT), :], b_buf.at[p], b_sem.at[p]).start()

    arrived(green_out.at[pl.ds(1, NROW - 1)], green_recv.at[0])

    for j in range(NB):
        source = target_ref[atom_ref[row * NB + j]] // NB
        block = green_in[source]
        green_all[j, here, :] = block[:SHARE]
        green_all[j, tail, :] = block[SHARE:]
    for o in (1, NDEP - 1):
        copy = pltpu.make_async_remote_copy(
            green_all.at[:, here, :], green_all.at[:, here, :], share_send.at[o // 11], share_recv.at[o // 11],
            device_id=(row, col, deps_of[o]), device_id_type=MESH,
        )
        copy.start()
        sent.append(copy)
    occ_copy.wait()
    for o in range(1, NCOL):
        copy = pltpu.make_async_remote_copy(
            occ_buf.at[:, pl.ds(mine, 128)], occ_buf.at[:, pl.ds(mine, 128)], occ_send.at[o], occ_recv.at[col],
            device_id=(row, cols_of[o], dep), device_id_type=MESH,
        )
        copy.start()
        sent.append(copy)
    before = pl.ds(pl.multiple_of(lax.rem(share + 2, 3) * SHARE, SHARE), SHARE)
    after = pl.ds(pl.multiple_of(lax.rem(share + 1, 3) * SHARE, SHARE), SHARE)
    arrived(green_all.at[:, before, :], share_recv.at[0])
    arrived(green_all.at[:, after, :], share_recv.at[1])

    parts = []
    for j in range(NB):
        atom = atom_ref[row * NB + j]
        kept = size_ref[atom] * screen_ref[atom]
        inside = lax.broadcasted_iota(jnp.int32, (KEPT, 128), 0) < kept
        parts.append(jnp.where(inside, green_all[j].astype(F32), 0.0).astype(BF16))
    rows_first = jnp.concatenate(parts, axis=0)
    green_ref[...] = rows_first.T


    def pair_copy(m):
        return pltpu.make_async_remote_copy(
            y_buf.at[2 * m + other], y_pair.at[m], pair_send.at[m], pair_recv.at[m],
            device_id=(row + 1 - 2 * core, col, dep), device_id_type=MESH,
        )

    def contract_first(m, owner):
        p = 2 * m + owner
        arrived(b_buf.at[p], b_sem.at[p])
        block = b_buf[p].reshape(NB * KEPT, BS)
        product = jnp.dot(green_ref[...], block, preferred_element_type=F32).astype(BF16).reshape(NY, 16, BS)
        y_buf[p] = product

    contract_first(0, other)
    pair_copy(0).start()

    @pl.loop(0, STEPS)
    def _(m):
        contract_first(m, core)

        @pl.when(m < STEPS - 1)
        def _():
            contract_first(m + 1, other)
            pair_copy(m + 1).start()

        pair_copy(m).wait_recv()
        y_out[m] = (y_buf[2 * m + core].astype(F32) + y_pair[m].astype(F32)).astype(BF16)
        for to in Y_ORDER:
            @pl.when(to != y)
            def _():
                pltpu.make_async_remote_copy(
                    y_out.at[m, to], y_in.at[m, y], y_send.at[0], y_recv.at[m],
                    device_id=(2 * to + core, col, dep), device_id_type=MESH,
                ).start()

        y_in[m, y] = y_out[m, y]

    for o in range(1, NCOL):
        piece = occ_buf.at[:, pl.ds(pl.multiple_of(cols_of[o] * 128, 128), 128)]
        arrived(piece, occ_recv.at[cols_of[o]])
    inside = lax.broadcasted_iota(jnp.int32, (BS, SIG), 0) < nu_ref[0]
    occ_kept[...] = jnp.where(inside, occ_buf[...].astype(F32), 0.0).astype(BF16)

    own = (core == parity) & (lax.rem(dep, 2) == core)
    @pl.loop(0, STEPS)
    def _(m):
        arrived(y_out.at[m, pl.ds(1, NY - 1)], y_recv.at[m])
        total = y_in[m, 0].astype(F32)
        for k in range(1, NY):
            total += y_in[m, k].astype(F32)
        w = jnp.dot(total.astype(BF16), occ_kept[...], preferred_element_type=F32).astype(BF16)
        for c in range(NCOL):
            w_out[m * NCOL + c] = w[:, c * 128 : (c + 1) * 128]
        @pl.loop(0, NCOL)
        def _(i):
            p = 2 * m + core
            slot = m * NCOL + i
            same = own & (dep == p) & (col == i)

            @pl.when(jnp.logical_not(same))
            def _():
                pltpu.make_async_remote_copy(
                    w_out.at[slot], w_in.at[dep * 2 + lax.rem(col, 2)], w_send.at[0], w_recv.at[0],
                    device_id=(2 * y + parity, i, p), device_id_type=MESH,
                ).start()

            @pl.when(same)
            def _():
                w_in[dep * 2 + lax.rem(col, 2)] = w_out[slot]

    @pl.when(own)
    def _():
        arrived(w_in.at[pl.ds(0, 2 * NDEP - 1)], w_recv.at[0])

    @pl.when(jnp.logical_not(own))
    def _():
        arrived(w_in, w_recv.at[0])

    for c in range(2):
        result = w_in[c].astype(F32)
        for k in range(1, NDEP):
            result += w_in[2 * k + c].astype(F32)
        out_ref[c] = result

    @pl.when(own)
    def _():
        arrived(w_out.at[pl.ds(0, 2 * NDEP - 1)], w_send.at[0])

    @pl.when(jnp.logical_not(own))
    def _():
        arrived(w_out, w_send.at[0])
    arrived(green_out.at[pl.ds(1, NROW - 1)], green_send.at[0])
    arrived(y_out.at[:, pl.ds(1, NY - 1)], y_send.at[0])
    for m in range(STEPS):
        pair_copy(m).wait_send()
    for copy in sent:
        copy.wait_send()


def body(b_tensor, occ_green, virt_green, mu_atom, mu_target, mu_sizes, nu_sizes, screen):
    smem = pl.BlockSpec(memory_space=pltpu.SMEM)
    hbm = pl.BlockSpec(memory_space=pl.ANY)
    dma = pltpu.SemaphoreType.DMA
    out = pl.pallas_call(
        kernel,
        name="contract",
        out_shape=jax.ShapeDtypeStruct((2, 16, 128), F32),
        in_specs=[smem] * 5 + [hbm] * 3,
        out_specs=pl.BlockSpec(memory_space=pltpu.VMEM),
        scratch_shapes=[
            pltpu.VMEM((NP, NB, KEPT, BS), BF16),
            pltpu.VMEM((NB, SHARE + TAIL, SIG), BF16),
            pltpu.VMEM((BS, SIG), BF16),
            pltpu.VMEM((BS, SIG), BF16),
            pltpu.VMEM((NB, SHARE + TAIL, 128), BF16),
            pltpu.VMEM((NROW, SHARE + TAIL, 128), BF16),
            pltpu.VMEM((NROW, SHARE + TAIL, 128), BF16),
            pltpu.VMEM((NB, KEPT, 128), BF16),
            pltpu.VMEM((128, NB * KEPT), BF16),
            pltpu.VMEM((NP, NY, 16, BS), BF16),
            pltpu.VMEM((STEPS, NY, 16, BS), BF16),
            pltpu.VMEM((STEPS, NY, 16, BS), BF16),
            pltpu.VMEM((STEPS, NY, 16, BS), BF16),
            pltpu.VMEM((STEPS * NCOL, 16, 128), BF16),
            pltpu.VMEM((2 * NDEP, 16, 128), BF16),
            dma((NP,)),
            dma((3,)),
            dma((1,)),
            dma((1,)),
            dma((2,)),
            dma((2,)),
            dma((NCOL,)),
            dma((NCOL,)),
            dma((STEPS,)),
            dma((STEPS,)),
            dma((1,)),
            dma((STEPS,)),
            dma((1,)),
            dma((1,)),
        ],
        compiler_params=pltpu.CompilerParams(
            collective_id=0, has_side_effects=True, vmem_limit_bytes=56 * 2**20
        ),
        cost_estimate=pl.CostEstimate(flops=1700000000, bytes_accessed=10000000, transcendentals=0),
    )(
        mu_atom,
        mu_target,
        mu_sizes,
        nu_sizes,
        screen.reshape(screen.shape[0]),
        b_tensor.reshape(NP, NB, BS, BS),
        virt_green.reshape(NB, BS, SIG),
        occ_green,
    )
    return out.reshape(SIG // NROW, 1, 128)


def solution(mesh):
    placed = (
        P(None, "row", "dep"),
        P("dep", "col"),
        P("row", None),
        P(),
        P(),
        P(),
        P("dep"),
        P(None, "dep"),
    )
    return jax.shard_map(
        body, mesh=mesh, in_specs=placed, out_specs=P("row", "dep", "col"), check_vma=False
    )
```

```python
import jax
import jax.numpy as jnp
from jax import lax
from jax.experimental import pallas as pl
from jax.experimental.pallas import tpu as pltpu
from jax.sharding import PartitionSpec as P

MESH = pl.DeviceIdType.MESH
BF16 = jnp.bfloat16
F32 = jnp.float32

BS = 256
NB = 6
KEPT = 208
SHARE = 64
TAIL = KEPT - 3 * SHARE
NROW, NCOL, NDEP = 16, 4, 12
NY = NROW // 2
NP = 12
SIG = 512
STEPS = NP // 2
Y_ORDER = (0, 1, 2, 7, 3, 6, 5, 4)
FAR_FIRST = (8, 9, 7, 10, 6, 11, 5, 12, 4, 13, 3, 14, 2, 15, 1)


def wrap(value, size):
    return jnp.where(value >= size, value - size, value)


def arrived(ref, sem):
    pltpu.make_async_copy(ref, ref, sem).wait()


def kernel(
    atom_ref,
    target_ref,
    size_ref,
    nu_ref,
    screen_ref,
    b_ref,
    virt_ref,
    occ_ref,
    out_ref,
    b_buf,
    virt_buf,
    occ_buf,
    occ_kept,
    picked,
    green_out,
    green_in,
    green_all,
    green_ref,
    y_buf,
    y_pair,
    y_out,
    y_in,
    w_out,
    w_in,
    b_sem,
    local_sem,
    green_send,
    green_recv,
    share_send,
    share_recv,
    occ_send,
    occ_recv,
    pair_send,
    pair_recv,
    y_send,
    y_recv,
    w_send,
    w_recv,
):
    row, col, dep = lax.axis_index("row"), lax.axis_index("col"), lax.axis_index("dep")
    core = lax.rem(row, 2)
    y = lax.div(row, 2)
    other = 1 - core
    parity = lax.div(col, 2)
    share = lax.rem(dep, 3)
    here = pl.ds(pl.multiple_of(share * SHARE, SHARE), SHARE)
    tail = pl.ds(3 * SHARE, TAIL)

    rows_of = [wrap(row + o, NROW) for o in range(NROW)]
    ys_of = [wrap(y + o, NY) for o in range(NY)]
    cols_of = [wrap(col + o, NCOL) for o in range(NCOL)]
    deps_of = [wrap(dep + o, NDEP) for o in range(NDEP)]
    virt_copies = [
        pltpu.make_async_copy(virt_ref.at[:, here, :], virt_buf.at[:, pl.ds(0, SHARE), :], local_sem.at[0]),
        pltpu.make_async_copy(virt_ref.at[:, tail, :], virt_buf.at[:, pl.ds(SHARE, TAIL), :], local_sem.at[1]),
    ]
    for copy in virt_copies:
        copy.start()
    barrier = pltpu.get_barrier_semaphore()
    for o in (5, 7, 4, 8, 3, 9, 2, 10, 1, 11):
        pl.semaphore_signal(barrier, inc=1, device_id=(row, col, deps_of[o]), device_id_type=MESH)
    for o in FAR_FIRST:
        pl.semaphore_signal(barrier, inc=1, device_id=(rows_of[o], col, dep), device_id_type=MESH)
    for o in range(1, NCOL):
        pl.semaphore_signal(barrier, inc=1, device_id=(row, cols_of[o], dep), device_id_type=MESH)

    q = lax.broadcasted_iota(jnp.int32, (1, 128), 1)
    column = (2 * (q >> 4) + parity) * 32 + lax.rem(col, 2) * 16 + (q & 15)
    choose = jnp.where(lax.broadcasted_iota(jnp.int32, (SIG, 128), 0) == column, 1.0, 0.0).astype(BF16)
    for copy in virt_copies:
        copy.wait()
    picked[...] = (
        jnp.dot(virt_buf[...].reshape(NB * (SHARE + TAIL), SIG), choose, preferred_element_type=F32)
        .astype(BF16)
        .reshape(NB, SHARE + TAIL, 128)
    )

    first = row * NB

    @pl.loop(0, NROW)
    def _(r):
        found = jnp.int32(0)
        for j in range(NB):
            t = target_ref[atom_ref[r * NB + j]] - first
            found += jnp.where((t >= 0) & (t < NB), t, 0)
        green_out[r] = picked[found]

    pl.semaphore_wait(barrier, NDEP + NROW + NCOL - 4)
    sent = []

    @pl.loop(0, NROW - 1)
    def _(i):
        o = jnp.where(lax.rem(i, 2) == 1, NY + lax.div(i + 1, 2), NY - lax.div(i, 2))
        to = wrap(row + o, NROW)
        pltpu.make_async_remote_copy(
            green_out.at[to], green_in.at[row], green_send.at[0], green_recv.at[0],
            device_id=(to, col, dep), device_id_type=MESH,
        ).start()

    green_in[row] = green_out[row]
    mine = pl.multiple_of(col * 128, 128)
    occ_copy = pltpu.make_async_copy(occ_ref, occ_buf.at[:, pl.ds(mine, 128)], local_sem.at[2])
    occ_copy.start()

    @pl.loop(0, NP)
    def _(p):
        pltpu.make_async_copy(b_ref.at[p, :, pl.ds(0, KEPT), :], b_buf.at[p], b_sem.at[p]).start()

    arrived(green_out.at[pl.ds(1, NROW - 1)], green_recv.at[0])

    for j in range(NB):
        source = target_ref[atom_ref[row * NB + j]] // NB
        block = green_in[source]
        green_all[j, here, :] = block[:SHARE]
        green_all[j, tail, :] = block[SHARE:]
    for o in (1, NDEP - 1):
        copy = pltpu.make_async_remote_copy(
            green_all.at[:, here, :], green_all.at[:, here, :], share_send.at[o // 11], share_recv.at[o // 11],
            device_id=(row, col, deps_of[o]), device_id_type=MESH,
        )
        copy.start()
        sent.append(copy)
    before = pl.ds(pl.multiple_of(lax.rem(share + 2, 3) * SHARE, SHARE), SHARE)
    after = pl.ds(pl.multiple_of(lax.rem(share + 1, 3) * SHARE, SHARE), SHARE)
    arrived(green_all.at[:, before, :], share_recv.at[0])
    arrived(green_all.at[:, after, :], share_recv.at[1])
    occ_copy.wait()
    for o in range(1, NCOL):
        copy = pltpu.make_async_remote_copy(
            occ_buf.at[:, pl.ds(mine, 128)], occ_buf.at[:, pl.ds(mine, 128)], occ_send.at[o], occ_recv.at[col],
            device_id=(row, cols_of[o], dep), device_id_type=MESH,
        )
        copy.start()
        sent.append(copy)

    parts = []
    for j in range(NB):
        atom = atom_ref[row * NB + j]
        kept = size_ref[atom] * screen_ref[atom]
        inside = lax.broadcasted_iota(jnp.int32, (KEPT, 128), 0) < kept
        parts.append(jnp.where(inside, green_all[j].astype(F32), 0.0).astype(BF16))
    rows_first = jnp.concatenate(parts, axis=0)
    green_ref[...] = rows_first.T


    def pair_copy(m):
        return pltpu.make_async_remote_copy(
            y_buf.at[2 * m + other], y_pair.at[m], pair_send.at[m], pair_recv.at[m],
            device_id=(row + 1 - 2 * core, col, dep), device_id_type=MESH,
        )

    def contract_first(m, owner):
        p = 2 * m + owner
        arrived(b_buf.at[p], b_sem.at[p])
        block = b_buf[p].reshape(NB * KEPT, BS)
        product = jnp.dot(green_ref[...], block, preferred_element_type=F32).astype(BF16).reshape(NY, 16, BS)
        y_buf[p] = product

    contract_first(0, other)
    pair_copy(0).start()

    @pl.loop(0, STEPS)
    def _(m):
        contract_first(m, core)

        @pl.when(m < STEPS - 1)
        def _():
            contract_first(m + 1, other)
            pair_copy(m + 1).start()

        pair_copy(m).wait_recv()
        y_out[m] = (y_buf[2 * m + core].astype(F32) + y_pair[m].astype(F32)).astype(BF16)
        for to in Y_ORDER:
            @pl.when(to != y)
            def _():
                pltpu.make_async_remote_copy(
                    y_out.at[m, to], y_in.at[m, y], y_send.at[0], y_recv.at[m],
                    device_id=(2 * to + core, col, dep), device_id_type=MESH,
                ).start()

        y_in[m, y] = y_out[m, y]

    for o in range(1, NCOL):
        piece = occ_buf.at[:, pl.ds(pl.multiple_of(cols_of[o] * 128, 128), 128)]
        arrived(piece, occ_recv.at[cols_of[o]])
    inside = lax.broadcasted_iota(jnp.int32, (BS, SIG), 0) < nu_ref[0]
    occ_kept[...] = jnp.where(inside, occ_buf[...].astype(F32), 0.0).astype(BF16)

    own = (core == parity) & (lax.rem(dep, 2) == core)
    @pl.loop(0, STEPS)
    def _(m):
        arrived(y_out.at[m, pl.ds(1, NY - 1)], y_recv.at[m])
        total = y_in[m, 0].astype(F32)
        for k in range(1, NY):
            total += y_in[m, k].astype(F32)
        w = jnp.dot(total.astype(BF16), occ_kept[...], preferred_element_type=F32).astype(BF16)
        for c in range(NCOL):
            w_out[m * NCOL + c] = w[:, c * 128 : (c + 1) * 128]
        @pl.loop(0, NCOL)
        def _(i):
            p = 2 * m + core
            slot = m * NCOL + i
            same = own & (dep == p) & (col == i)

            @pl.when(jnp.logical_not(same))
            def _():
                pltpu.make_async_remote_copy(
                    w_out.at[slot], w_in.at[dep * 2 + lax.rem(col, 2)], w_send.at[0], w_recv.at[0],
                    device_id=(2 * y + parity, i, p), device_id_type=MESH,
                ).start()

            @pl.when(same)
            def _():
                w_in[dep * 2 + lax.rem(col, 2)] = w_out[slot]

    @pl.when(own)
    def _():
        arrived(w_in.at[pl.ds(0, 2 * NDEP - 1)], w_recv.at[0])

    @pl.when(jnp.logical_not(own))
    def _():
        arrived(w_in, w_recv.at[0])

    for c in range(2):
        result = w_in[c].astype(F32)
        for k in range(1, NDEP):
            result += w_in[2 * k + c].astype(F32)
        out_ref[c] = result

    @pl.when(own)
    def _():
        arrived(w_out.at[pl.ds(0, 2 * NDEP - 1)], w_send.at[0])

    @pl.when(jnp.logical_not(own))
    def _():
        arrived(w_out, w_send.at[0])
    arrived(green_out.at[pl.ds(1, NROW - 1)], green_send.at[0])
    arrived(y_out.at[:, pl.ds(1, NY - 1)], y_send.at[0])
    for m in range(STEPS):
        pair_copy(m).wait_send()
    for copy in sent:
        copy.wait_send()


def body(b_tensor, occ_green, virt_green, mu_atom, mu_target, mu_sizes, nu_sizes, screen):
    smem = pl.BlockSpec(memory_space=pltpu.SMEM)
    hbm = pl.BlockSpec(memory_space=pl.ANY)
    dma = pltpu.SemaphoreType.DMA
    out = pl.pallas_call(
        kernel,
        name="contract",
        out_shape=jax.ShapeDtypeStruct((2, 16, 128), F32),
        in_specs=[smem] * 5 + [hbm] * 3,
        out_specs=pl.BlockSpec(memory_space=pltpu.VMEM),
        scratch_shapes=[
            pltpu.VMEM((NP, NB, KEPT, BS), BF16),
            pltpu.VMEM((NB, SHARE + TAIL, SIG), BF16),
            pltpu.VMEM((BS, SIG), BF16),
            pltpu.VMEM((BS, SIG), BF16),
            pltpu.VMEM((NB, SHARE + TAIL, 128), BF16),
            pltpu.VMEM((NROW, SHARE + TAIL, 128), BF16),
            pltpu.VMEM((NROW, SHARE + TAIL, 128), BF16),
            pltpu.VMEM((NB, KEPT, 128), BF16),
            pltpu.VMEM((128, NB * KEPT), BF16),
            pltpu.VMEM((NP, NY, 16, BS), BF16),
            pltpu.VMEM((STEPS, NY, 16, BS), BF16),
            pltpu.VMEM((STEPS, NY, 16, BS), BF16),
            pltpu.VMEM((STEPS, NY, 16, BS), BF16),
            pltpu.VMEM((STEPS * NCOL, 16, 128), BF16),
            pltpu.VMEM((2 * NDEP, 16, 128), BF16),
            dma((NP,)),
            dma((3,)),
            dma((1,)),
            dma((1,)),
            dma((2,)),
            dma((2,)),
            dma((NCOL,)),
            dma((NCOL,)),
            dma((STEPS,)),
            dma((STEPS,)),
            dma((1,)),
            dma((STEPS,)),
            dma((1,)),
            dma((1,)),
        ],
        compiler_params=pltpu.CompilerParams(
            collective_id=0, has_side_effects=True, vmem_limit_bytes=56 * 2**20
        ),
        cost_estimate=pl.CostEstimate(flops=1700000000, bytes_accessed=10000000, transcendentals=0),
    )(
        mu_atom,
        mu_target,
        mu_sizes,
        nu_sizes,
        screen.reshape(screen.shape[0]),
        b_tensor.reshape(NP, NB, BS, BS),
        virt_green.reshape(NB, BS, SIG),
        occ_green,
    )
    return out.reshape(SIG // NROW, 1, 128)


def solution(mesh):
    placed = (
        P(None, "row", "dep"),
        P("dep", "col"),
        P("row", None),
        P(),
        P(),
        P(),
        P("dep"),
        P(None, "dep"),
    )
    return jax.shard_map(
        body, mesh=mesh, in_specs=placed, out_specs=P("row", "dep", "col"), check_vma=False
    )
```
